32 devices in a mesh: seq: 8 (over z, y), res: 4 (over x, core).
Axes of the slice: x: 2, y: 2, z: 4, core: 2. Of those that a mesh axis runs over, the one named last changes fastest.
Arguments:
- alignment_query: bfloat16 [64, 256, 256], P(('seq', 'res')), may hold values from -8 to 8
- alignment_key: bfloat16 [64, 256, 256], P(('seq', 'res')), may hold values from -8 to 8
- attended_vectors: bfloat16 [64, 256, 256], P(('seq', 'res')), may hold values from -6 to 6
- attended_cotangent: bfloat16 [64, 256, 256], P(('seq', 'res')), may hold values from -6 to 6
- chain_index_per_residue: int32 [256], replicated, may hold values from 0 to 3, as said below
- pair: bfloat16 [256, 256, 128], P('res', 'seq'), may hold values from -6 to 6
- pair_bias_matrix: bfloat16 [128, 8], replicated, may hold values from -0.5 to 0.5
- left_operand_input: bfloat16 [256, 256, 128], P('seq', 'res'), may hold values from -6 to 6
- right_operand_input: bfloat16 [256, 256, 128], P('res', 'seq'), may hold values from -6 to 6
Outputs:
- query_gradient: bfloat16 [64, 256, 256], P(('seq', 'res'))
- key_gradient: bfloat16 [64, 256, 256], P(('seq', 'res'))
- value_gradient: bfloat16 [64, 256, 256], P(('seq', 'res'))
- d_bias_weight: float32 [128, 8], replicated
- d_left: bfloat16 [256, 256, 128], P('seq', 'res')
- d_right: bfloat16 [256, 256, 128], P('res', 'seq')
The draws below stay inside these ranges and needn't reach their ends.
Inputs may be any that keep to these rules, and one draw needn't show every extreme that they name: `chain_index_per_residue`: chain numbers never fall along the residues; four chains, each of at least 32 residues.
All inputs are finite; a program needn't handle non-finite values.
Results may differ from the reference program's by a relative error of at most 0.0074.
Values may be sent and summed in bfloat16 or wider, within the bound.
No kernel may reach another device: no remote copies, remote signals or barrier semaphores. Data moves between devices by JAX's collectives and lax.ppermute only.
A program may use at most 64 MiB of HBM per device.

```python
import jax
import jax.numpy as jnp
from jax import lax

HEADS = 8
HEAD_DIM = 32
PAIR = 128
WINDOW_AMINOS = 256
EMBED_CHANNELS = 256
HOMOLOG_COUNT = 64
N_SEQ = 8
N_RES = 4


def draw_alignment_query(key, part):
    content_entries = jnp.clip(jax.random.normal(jax.random.fold_in(key, 1), (HOMOLOG_COUNT, WINDOW_AMINOS, EMBED_CHANNELS), jnp.float32), -6.0, 6.0)
    return content_entries.astype(jnp.bfloat16)


def draw_alignment_key(key, part):
    content_entries = jnp.clip(jax.random.normal(jax.random.fold_in(key, 2), (HOMOLOG_COUNT, WINDOW_AMINOS, EMBED_CHANNELS), jnp.float32), -6.0, 6.0)
    return content_entries.astype(jnp.bfloat16)


def draw_chain_index_per_residue(key, part):
    offsets = jax.random.randint(jax.random.fold_in(key, 4), (3,), -(WINDOW_AMINOS // 16), WINDOW_AMINOS // 16 + 1)
    cuts = (jnp.arange(1, 4, dtype=jnp.int32) * (WINDOW_AMINOS // 4) + offsets).astype(jnp.int32)
    positions = jnp.arange(WINDOW_AMINOS, dtype=jnp.int32)
    return jnp.sum((positions[:, None] >= cuts[None, :]).astype(jnp.int32), axis=1).astype(jnp.int32)


def raised(result, own_key, source, target, shards_of, factor):
    owner, partner = [(jnp.arange(result.shape[dim]) // (result.shape[dim] // shards_of)).reshape([-1 if axis == dim else 1 for axis in range(result.ndim)]) for dim in (source, target)]
    chosen = jax.random.permutation(own_key, shards_of)[partner]
    strong = (owner == chosen) | (owner == (partner + shards_of // 2) % shards_of)
    return jnp.where(strong, factor * result, result)


def level_of(key, shape, cuts, low, largest):
    def one(position, shards_of):
        draws = jax.random.uniform(jax.random.fold_in(jax.random.fold_in(key, 6), position), (shards_of,), jnp.float32, low / len(cuts), largest / len(cuts))
        return jnp.repeat(jnp.exp(draws), shape[position] // shards_of).reshape((-1,) + (1,) * (len(shape) - position - 1))

    gain = one(*cuts[0])
    for cut in cuts[1:]:
        gain = gain * one(*cut)
    return gain


def scatter_about(rng, shape, width, most, pieces=(), held_as=jnp.bfloat16):
    values = jax.random.normal(rng, shape, jnp.float32) * width
    if len(pieces) > 0:
        values = level_of(rng, shape, pieces, -0.22, 0.18) * values
    return jnp.clip(values, min=-most, max=most).astype(held_as)


def gaussian_with(stream_key, dims, deviation, reach, pieces, heavy, kind=jnp.bfloat16):
    array = deviation * jax.random.normal(stream_key, dims, jnp.float32)
    if pieces:
        array = array * level_of(stream_key, dims, pieces, -0.22, 0.18)
    return jnp.clip(raised(array, jax.random.fold_in(stream_key, 3), *heavy), -reach, reach).astype(kind)


def setup_inputs(seed: int = 0) -> dict:
    arg_keys = jax.random.split(jax.random.key(seed), 10)
    alignment_query = draw_alignment_query(jax.random.fold_in(arg_keys[9], 71), 0)
    alignment_key = draw_alignment_key(jax.random.fold_in(arg_keys[9], 71), 0)
    attended_vectors = scatter_about(arg_keys[2], (HOMOLOG_COUNT, WINDOW_AMINOS, EMBED_CHANNELS), 1.0, 6.0, ((0, 32),))
    attended_cotangent = gaussian_with(arg_keys[3], (HOMOLOG_COUNT, WINDOW_AMINOS, EMBED_CHANNELS), 1.0, 6.0, ((0, 32),), (0, 1, 32, 2.75))
    chain_index_per_residue = draw_chain_index_per_residue(jax.random.fold_in(arg_keys[9], 71), 0)
    pair = scatter_about(arg_keys[5], (WINDOW_AMINOS, WINDOW_AMINOS, PAIR), 1.0, 6.0, ((0, 4), (1, 8)))
    pair_bias_matrix = scatter_about(arg_keys[6], (PAIR, HEADS), PAIR ** -0.5, 0.5)
    left_operand_input = scatter_about(arg_keys[7], (WINDOW_AMINOS, WINDOW_AMINOS, PAIR), 1.0, 6.0, ((0, 8), (1, 4)))
    right_operand_input = scatter_about(arg_keys[8], (WINDOW_AMINOS, WINDOW_AMINOS, PAIR), 1.0, 6.0, ((0, 4), (1, 8)))
    return dict(alignment_query=alignment_query, alignment_key=alignment_key, attended_vectors=attended_vectors, attended_cotangent=attended_cotangent, chain_index_per_residue=chain_index_per_residue, pair=pair, pair_bias_matrix=pair_bias_matrix, left_operand_input=left_operand_input, right_operand_input=right_operand_input)


big_negative = -1e30


def reference(alignment_query, alignment_key, attended_vectors, attended_cotangent, chain_index_per_residue, pair, pair_bias_matrix, left_operand_input, right_operand_input):
    f32 = jnp.float32
    reduced_mantissa_type = jnp.bfloat16
    logit_multiplier = HEAD_DIM ** -0.5
    rows_group = WINDOW_AMINOS // N_RES
    cols_group = WINDOW_AMINOS // N_SEQ
    bias = jnp.einsum('ijc,ch->hij', pair.astype(f32), pair_bias_matrix.astype(f32), precision=lax.Precision.HIGHEST)
    allowed = chain_index_per_residue[:, None] == chain_index_per_residue[None, :]

    def single_row(carry, row):
        query, keys, content_entries, grads = row
        asking_vectors_unit = query.astype(f32).reshape(WINDOW_AMINOS, HEADS, HEAD_DIM)
        lookup_vectors_unit = keys.astype(f32).reshape(WINDOW_AMINOS, HEADS, HEAD_DIM)
        vh = content_entries.astype(f32).reshape(WINDOW_AMINOS, HEADS, HEAD_DIM)
        attention_unit_cotangent = grads.astype(f32).reshape(WINDOW_AMINOS, HEADS, HEAD_DIM)
        scores = jnp.einsum('ihd,jhd->hij', asking_vectors_unit, lookup_vectors_unit) * logit_multiplier + bias
        scores = jnp.where(allowed[None], scores, big_negative)
        top = jnp.max(scores, axis=-1, keepdims=True)
        expo = jnp.exp(scores - top)
        probs = expo / jnp.sum(expo, axis=-1, keepdims=True)
        dprobs = jnp.einsum('ihd,jhd->hij', attention_unit_cotangent, vh)
        dscores = probs * (dprobs - jnp.sum(probs * dprobs, axis=-1, keepdims=True))
        logit_cotangent_coarse = dscores.astype(reduced_mantissa_type).astype(f32)
        softmax_weights_coarse = probs.astype(reduced_mantissa_type).astype(f32)
        asking_cotangent_unit = (jnp.einsum('ayw,wak->yak', logit_cotangent_coarse, lookup_vectors_unit) * logit_multiplier).astype(reduced_mantissa_type).reshape(WINDOW_AMINOS, EMBED_CHANNELS)
        lookup_cotangent_unit = (jnp.einsum('lzx,zlf->xlf', logit_cotangent_coarse, asking_vectors_unit) * logit_multiplier).astype(reduced_mantissa_type).reshape(WINDOW_AMINOS, EMBED_CHANNELS)
        content_cotangent_unit = jnp.einsum('lzx,zlf->xlf', softmax_weights_coarse, attention_unit_cotangent).astype(reduced_mantissa_type).reshape(WINDOW_AMINOS, EMBED_CHANNELS)
        return carry + dscores, (asking_cotangent_unit, lookup_cotangent_unit, content_cotangent_unit)

    start_offset = jnp.zeros((HEADS, WINDOW_AMINOS, WINDOW_AMINOS), jnp.float32)
    bias_gradient, (query_gradient, key_gradient, value_gradient) = lax.scan(single_row, start_offset, (alignment_query, alignment_key, attended_vectors, attended_cotangent))
    d_bias_weight = jnp.einsum('ijc,hij->ch', pair.astype(f32), bias_gradient, precision=lax.Precision.HIGHEST)
    pair_grad = jnp.einsum('hij,ch->ijc', bias_gradient, pair_bias_matrix.astype(f32), precision=lax.Precision.HIGHEST).astype(reduced_mantissa_type)

    def left_group(index, total):
        first = (jnp.asarray(index, jnp.int32) * cols_group).astype(jnp.int32)
        right_piece = lax.dynamic_slice_in_dim(right_operand_input, first, cols_group, 1).astype(f32)
        grad_piece = lax.dynamic_slice_in_dim(pair_grad, first, cols_group, 1).astype(f32)
        return total + jnp.einsum('kjc,ijc->kic', right_piece, grad_piece, precision=lax.Precision.HIGHEST)

    def right_group(index, total):
        first = (jnp.asarray(index, jnp.int32) * rows_group).astype(jnp.int32)
        left_piece = lax.dynamic_slice_in_dim(left_operand_input, first, rows_group, 1).astype(f32)
        grad_piece = lax.dynamic_slice_in_dim(pair_grad, first, rows_group, 0).astype(f32)
        return total + jnp.einsum('kic,ijc->kjc', left_piece, grad_piece, precision=lax.Precision.HIGHEST)

    empty = jnp.zeros((WINDOW_AMINOS, WINDOW_AMINOS, PAIR), jnp.float32)
    d_left = lax.fori_loop(0, N_SEQ, left_group, empty).astype(reduced_mantissa_type)
    d_right = lax.fori_loop(0, N_RES, right_group, empty).astype(reduced_mantissa_type)
    return query_gradient, key_gradient, value_gradient, d_bias_weight, d_left, d_right
```

```python
import functools
import math

import jax
import jax.numpy as jnp
from jax import lax
from jax.experimental import pallas as pl
from jax.experimental.pallas import tpu as pltpu
from jax.sharding import PartitionSpec as P

HEADS = 8
HEAD_DIM = 32
BIG_NEGATIVE = -1e30
BOTH = ("seq", "res")
NT = (((1,), (1,)), ((), ()))
TN = (((0,), (0,)), ((), ()))

f32 = jnp.float32
bf16 = jnp.bfloat16


def attention_kernel(
    n_seq, n_res, x_ref, bias_ref, chain_row_ref, chain_col_ref, grads_ref, share_ref, masked, total
):
    step = pl.program_id(0)
    heads, residues, _ = masked.shape
    cols, rows = residues // n_seq, residues // n_res
    width = heads * HEAD_DIM
    scale = HEAD_DIM**-0.5

    @pl.when(step == 0)
    def _():
        for h in range(heads):
            for a in range(n_seq):
                band = jnp.concatenate(
                    [bias_ref[a * n_res + b, :, h * rows : (h + 1) * rows] for b in range(n_res)],
                    axis=-1,
                )
                allowed = chain_col_ref[a * cols : (a + 1) * cols, :] == chain_row_ref[...]
                masked[h, a * cols : (a + 1) * cols, :] = jnp.where(allowed, band, BIG_NEGATIVE)
        total[...] = jnp.zeros_like(total)

    query_parts, key_parts, value_parts = [], [], []
    for h in range(heads):
        q, k, v, g = [
            x_ref[0, :, t * width + h * HEAD_DIM : t * width + (h + 1) * HEAD_DIM] for t in range(4)
        ]
        scores = lax.dot_general(k, q, NT, preferred_element_type=f32) * scale + masked[h]
        top = jnp.max(scores, axis=0, keepdims=True)
        expo = jnp.exp(scores - top)
        probs = expo * (1.0 / jnp.sum(expo, axis=0, keepdims=True))
        dprobs = lax.dot_general(v, g, NT, preferred_element_type=f32)
        dscores = probs * (dprobs - jnp.sum(probs * dprobs, axis=0, keepdims=True))
        total[h] += dscores
        dscores_b = dscores.astype(bf16)
        query_parts.append(lax.dot_general(dscores_b, k, TN, preferred_element_type=f32) * scale)
        key_parts.append(jnp.dot(dscores_b, q, preferred_element_type=f32) * scale)
        value_parts.append(jnp.dot(probs.astype(bf16), g, preferred_element_type=f32))
    grads_ref[0] = jnp.concatenate(query_parts + key_parts + value_parts, axis=-1).astype(bf16)

    @pl.when(step == pl.num_programs(0) - 1)
    def _():
        for a in range(n_seq):
            for b in range(n_res):
                share_ref[a * n_res + b] = jnp.concatenate(
                    [
                        total[h, a * cols : (a + 1) * cols, b * rows : (b + 1) * rows]
                        for h in range(heads)
                    ],
                    axis=-1,
                ).astype(bf16)


def triangle_kernel(
    n_seq, n_res, bias_grad_ref, weight_ref, left_ref, right_ref, d_left_ref, d_right_ref, flat, turned
):
    heads, residues, _ = flat.shape
    groups = bias_grad_ref.shape[1]
    held = heads // groups
    cols, rows = residues // n_seq, residues // n_res
    for h in range(heads):
        group, place = h // held, h % held
        for a in range(n_seq):
            turned[h, a * cols : (a + 1) * cols, :] = jnp.concatenate(
                [
                    bias_grad_ref[a * n_res + b, group, :, place * rows : (place + 1) * rows]
                    for b in range(n_res)
                ],
                axis=-1,
            )
        flat[h] = turned[h].astype(f32).T.astype(bf16)
    for operand, grad, out in ((right_ref, flat, d_left_ref), (left_ref, turned, d_right_ref)):
        for k in range(operand.shape[0]):
            row = jnp.zeros(operand.shape[1:], f32)
            for h in range(heads):
                product = jnp.dot(grad[h], operand[k], preferred_element_type=f32)
                row += product * weight_ref[h : h + 1, :]
            out[k] = row.astype(bf16)


def shards(
    n_seq,
    n_res,
    alignment_query,
    alignment_key,
    attended_vectors,
    attended_cotangent,
    chain_index_per_residue,
    pair,
    pair_bias_matrix,
    left_operand_input,
    right_operand_input,
):
    own, residues, channels = alignment_query.shape
    devices = n_seq * n_res
    groups = math.gcd(HEADS, n_res)
    held = HEADS // groups
    width = held * HEAD_DIM
    rows, cols, pair_channels = pair.shape
    sequences = own * groups
    index_groups = None
    if groups != n_res:
        index_groups = [list(range(s, s + groups)) for s in range(0, n_res, groups)]

    def over_heads(x):
        return lax.all_to_all(x, "res", 0, 0, axis_index_groups=index_groups, tiled=True)

    bias = jnp.einsum("ijc,ch->hij", pair, pair_bias_matrix, preferred_element_type=f32)
    bias = bias.reshape(groups, held, rows, cols).transpose(0, 3, 1, 2)
    bias = bias.reshape(groups, cols, held * rows)
    bias = jnp.broadcast_to(bias[None], (devices // groups, groups, cols, held * rows))
    bias = lax.all_to_all(
        bias.reshape(devices, cols, held * rows), BOTH, 0, 0, tiled=True
    )

    arrays = jnp.stack([alignment_query, alignment_key, attended_vectors, attended_cotangent])
    arrays = arrays.reshape(4, own, residues, groups, width).transpose(3, 1, 2, 0, 4)
    arrays = over_heads(arrays.reshape(sequences, residues, 4 * width))

    left_rows = lax.all_to_all(left_operand_input, "res", 0, 1, tiled=True)
    left_rows = lax.ppermute(
        left_rows, BOTH, [(d, (d % n_seq) * n_res + d // n_seq) for d in range(devices)]
    )
    right_rows = lax.all_to_all(right_operand_input, "seq", 0, 1, tiled=True)
    right_rows = lax.ppermute(
        right_rows, BOTH, [((d % n_seq) * n_res + d // n_seq, d) for d in range(devices)]
    )

    whole = lambda shape: pl.BlockSpec(shape, lambda s: (0,) * len(shape))
    grads, share = pl.pallas_call(
        functools.partial(attention_kernel, n_seq, n_res),
        grid=(sequences,),
        in_specs=[
            pl.BlockSpec((1, residues, 4 * width), lambda s: (s, 0, 0)),
            whole(bias.shape),
            whole((1, residues)),
            whole((residues, 1)),
        ],
        out_specs=[
            pl.BlockSpec((1, residues, 3 * width), lambda s: (s, 0, 0)),
            whole(bias.shape),
        ],
        out_shape=[
            jax.ShapeDtypeStruct((sequences, residues, 3 * width), bf16),
            jax.ShapeDtypeStruct(bias.shape, bf16),
        ],
        scratch_shapes=[pltpu.VMEM((held, residues, residues), f32)] * 2,
        compiler_params=pltpu.CompilerParams(vmem_limit_bytes=32 * 1024 * 1024),
        name="attention",
    )(
        arrays,
        bias,
        chain_index_per_residue.reshape(1, residues),
        chain_index_per_residue.reshape(residues, 1),
    )

    share = lax.all_to_all(share, BOTH, 0, 0, tiled=True)
    block = jnp.sum(
        share.astype(f32).reshape(devices // groups, groups, cols, held * rows), axis=0
    )
    bias_grad = jnp.broadcast_to(block.astype(bf16)[None], (devices,) + block.shape)
    bias_grad = lax.all_to_all(bias_grad, BOTH, 0, 0, tiled=True)

    own_grad = block.reshape(groups, cols, held, rows).transpose(0, 2, 3, 1)
    own_grad = own_grad.reshape(HEADS, rows, cols)
    weight_term = jnp.einsum(
        "ijc,hij->ch", pair.astype(f32), own_grad, precision=lax.Precision.HIGHEST
    )
    d_bias_weight = lax.psum(weight_term, BOTH)

    share_rows = left_rows.shape
    d_left, d_right = pl.pallas_call(
        functools.partial(triangle_kernel, n_seq, n_res),
        out_shape=[jax.ShapeDtypeStruct(share_rows, bf16)] * 2,
        scratch_shapes=[pltpu.VMEM((HEADS, residues, residues), bf16)] * 2,
        compiler_params=pltpu.CompilerParams(vmem_limit_bytes=32 * 1024 * 1024),
        name="triangle",
    )(bias_grad, pair_bias_matrix.astype(f32).T, left_rows, right_rows)
    d_left = lax.all_to_all(d_left, "res", 1, 0, tiled=True)
    d_right = lax.all_to_all(d_right, "seq", 1, 0, tiled=True)

    grads = over_heads(grads).reshape(groups, own, residues, 3, width)
    grads = grads.transpose(3, 1, 2, 0, 4).reshape(3, own, residues, channels)
    return (grads[0], grads[1], grads[2], d_bias_weight, d_left, d_right)


def solution(mesh):
    placed = (
        P(BOTH, None, None),
        P(BOTH, None, None),
        P(BOTH, None, None),
        P(BOTH, None, None),
        P(),
        P("res", "seq", None),
        P(),
        P("seq", "res", None),
        P("res", "seq", None),
    )
    return jax.shard_map(
        functools.partial(shards, mesh.shape["seq"], mesh.shape["res"]),
        mesh=mesh,
        in_specs=placed,
        out_specs=(
            P(BOTH, None, None),
            P(BOTH, None, None),
            P(BOTH, None, None),
            P(),
            P("seq", "res", None),
            P("res", "seq", None),
        ),
        check_vma=False,
    )
```

```python
import functools
import math

import jax
import jax.numpy as jnp
from jax import lax
from jax.experimental import pallas as pl
from jax.experimental.pallas import tpu as pltpu
from jax.sharding import PartitionSpec as P

HEADS = 8
HEAD_DIM = 32
BIG_NEGATIVE = -1e30
BOTH = ("seq", "res")
NT = (((1,), (1,)), ((), ()))
TN = (((0,), (0,)), ((), ()))

f32 = jnp.float32
bf16 = jnp.bfloat16


def attention_kernel(
    n_seq, n_res, groups, bias_ref, chain_ref, *refs
):
    arrays, grads = refs[:groups], refs[groups : 2 * groups]
    share_ref, masked, total = refs[2 * groups :]
    heads, residues, _ = masked.shape
    cols, rows = residues // n_seq, residues // n_res
    width = heads * HEAD_DIM
    scale = HEAD_DIM**-0.5

    chain_row = chain_ref[...].astype(f32)
    chain_col = jnp.broadcast_to(chain_row, (8, residues)).T[:, :1]
    for h in range(heads):
        for a in range(n_seq):
            band = jnp.concatenate(
                [bias_ref[a * n_res + b, :, h * rows : (h + 1) * rows] for b in range(n_res)],
                axis=-1,
            )
            allowed = chain_col[a * cols : (a + 1) * cols] == chain_row
            masked[h, a * cols : (a + 1) * cols, :] = jnp.where(allowed, band, BIG_NEGATIVE)
    total[...] = jnp.zeros_like(total)

    def sequence(x_ref, n):
        query_parts, key_parts, value_parts = [], [], []
        for h in range(heads):
            q, k, v, g = [
                x_ref[n, :, t * width + h * HEAD_DIM : t * width + (h + 1) * HEAD_DIM]
                for t in range(4)
            ]
            scores = lax.dot_general(k, q, NT, preferred_element_type=f32) * scale + masked[h]
            top = jnp.max(scores, axis=0, keepdims=True)
            expo = jnp.exp(scores - top)
            probs = expo * (1.0 / jnp.sum(expo, axis=0, keepdims=True))
            dprobs = lax.dot_general(v, g, NT, preferred_element_type=f32)
            dscores = probs * (dprobs - jnp.sum(probs * dprobs, axis=0, keepdims=True))
            total[h] += dscores
            dscores_b = dscores.astype(bf16)
            query_parts.append(
                lax.dot_general(dscores_b, k, TN, preferred_element_type=f32) * scale
            )
            key_parts.append(jnp.dot(dscores_b, q, preferred_element_type=f32) * scale)
            value_parts.append(jnp.dot(probs.astype(bf16), g, preferred_element_type=f32))
        return [
            jnp.concatenate(parts, axis=-1).astype(bf16)
            for parts in (query_parts, key_parts, value_parts)
        ]

    for s in range(groups):
        units = sum([sequence(arrays[s], n) for n in range(arrays[s].shape[0])], [])
        slots = grads[s].shape[0]
        each = len(units) // slots
        for n in range(slots):
            grads[s][n] = jnp.concatenate(units[n * each : (n + 1) * each], axis=-1)

    for a in range(n_seq):
        for b in range(n_res):
            share_ref[a * n_res + b] = jnp.concatenate(
                [
                    total[h, a * cols : (a + 1) * cols, b * rows : (b + 1) * rows]
                    for h in range(heads)
                ],
                axis=-1,
            ).astype(bf16)


def unpack_kernel(place_ref, *refs):
    pieces, outs, held = refs[:-4], refs[-4:-1], refs[-1]
    groups = len(pieces)
    own = outs[0].shape[0]
    slots, _, lanes = pieces[0].shape
    each = 3 * own // slots
    width = lanes // each
    for s in range(groups):
        held[s] = pieces[s][...]
    place = place_ref[0]
    for t in range(3):
        for n in range(own):
            slot, start = (3 * n + t) // each, (3 * n + t) % each * width
            outs[t][n] = jnp.concatenate(
                [held[place ^ g, slot, :, start : start + width] for g in range(groups)], axis=-1
            )


def pack_kernel(groups, n_res, scalars, chain_ref, *refs):
    arrays, (left_ref, right_ref), refs = refs[:4], refs[4:6], refs[6:]
    chain_out, outs, triangles = refs[0], refs[1 : 1 + groups], refs[1 + groups : -4]
    whole, held, loaded, sent = refs[-4:]
    place, b = scalars[0], scalars[1]
    block, rows = triangles[0].shape[1:3]
    cols = right_ref.shape[-2]
    loads = [
        pltpu.make_async_copy(x, whole.at[n], loaded.at[n]) for n, x in enumerate(arrays)
    ]
    for load in loads:
        load.start()
    copies = []
    for s in range(n_res):
        t = turn(b ^ s, n_res) * block
        copies.append((left_ref.at[pl.ds(t, block)], triangles[s].at[0]))
        for y in range(rows // cols):
            copies.append(
                (right_ref.at[y, b ^ s], triangles[s].at[1, :, y * cols : (y + 1) * cols])
            )
    copies = [pltpu.make_async_copy(x, y, sent.at[n]) for n, (x, y) in enumerate(copies)]
    for copy in copies:
        copy.start()
    chain_out[...] = chain_ref[...]
    for load in loads:
        load.wait()
    width = whole.shape[-1] // groups
    for g in range(groups):
        held[g] = jnp.concatenate(
            [whole[n, :, :, g * width : (g + 1) * width] for n in range(4)], axis=-1
        )
    for s in range(groups):
        outs[s][...] = held[place ^ s]
    for copy in copies:
        copy.wait()


def turn(b, n_res):
    return b % 2 * (n_res // 2) + b // 2


def order_kernel(scalars, *refs):
    pieces, (left_ref, chunks_ref) = refs[:-2], refs[-2:]
    rows, cols = pieces[0].shape[2], chunks_ref.shape[2]
    each = rows // cols
    for s, piece in enumerate(pieces):
        b = scalars[0] ^ s
        left_ref[:, pl.ds(pl.multiple_of(b * rows, rows), rows), :] = piece[0]
        for y in range(each):
            chunks_ref[b * each + y] = piece[1, :, y * cols : (y + 1) * cols]


def d_left_kernel(n_seq, n_res, scalars, near_ref, extra_ref, *refs):
    rights, outs = refs[:2], refs[2:-2]
    flat, right = refs[-2:]
    heads, count, residues = flat.shape
    held = heads // near_ref.shape[1]
    cols, rows = residues // n_seq, residues // n_res
    across = n_res // 2
    block = rights[0].shape[1]
    core, x = scalars[0], scalars[1]
    for part in range(2):
        where = core ^ part
        for a in range(n_seq):
            right[where, :, a * cols : (a + 1) * cols, :] = rights[part][a]
    for h in range(heads):
        group, place = h // held, h % held
        turned = jnp.concatenate(
            [
                jnp.concatenate(
                    [
                        near_ref[a * across + u, group, :, place * rows : (place + 1) * rows]
                        for u in range(across)
                    ],
                    axis=-1,
                )
                for a in range(n_seq)
            ],
            axis=0,
        )
        flat[h] = turned.astype(f32).T.astype(bf16)
    sums = outs[-1]
    for c in range(2):
        for k in range(block):
            row = jnp.zeros((count, right.shape[-1]), f32)
            for h in range(heads):
                product = jnp.dot(flat[h], right[c, k], preferred_element_type=f32)
                row += product * extra_ref[0, h : h + 1, :]
            for u in range(across):
                sums[u, c * block + k] = row[u * rows : (u + 1) * rows].astype(bf16)
    for s in range(across):
        outs[s][...] = sums[x ^ s]


def d_right_kernel(n_seq, n_res, scalars, near_ref, far_ref, extra_ref, left, out, turned):
    heads, residues, _ = turned.shape
    held = heads // near_ref.shape[1]
    cols, rows = residues // n_seq, residues // n_res
    across = n_res // 2
    block = left.shape[0]
    core = scalars[0]
    for h in range(heads):
        group, place = h // held, h % held
        for a in range(n_seq):
            band = []
            for b in range(n_res):
                piece = (
                    a * across + b // 2, group, slice(None), slice(place * rows, (place + 1) * rows)
                )
                band.append(jnp.where(core == b % 2, near_ref[piece], far_ref[piece]))
            turned[h, a * cols : (a + 1) * cols, :] = jnp.concatenate(band, axis=-1)
    for k in range(block):
        row = jnp.zeros((residues, left.shape[-1]), f32)
        for h in range(heads):
            product = jnp.dot(turned[h], left[k], preferred_element_type=f32)
            row += product * extra_ref[0, h : h + 1, :]
        for a in range(n_seq):
            out[a, k * cols : (k + 1) * cols] = row[a * cols : (a + 1) * cols].astype(bf16)
    term = extra_ref[1]
    high = term.astype(bf16).astype(f32)
    both = jnp.concatenate([high, term - high], axis=0).astype(bf16)
    for a in range(n_seq):
        out[a, block * cols :] = both


def place_kernel(inner, scalars, received_ref, *refs):
    pieces, (term_ref, left_ref, right_ref) = refs[:-3], refs[-3:]
    heads = term_ref.shape[0]
    sources, size, _ = received_ref.shape
    cols = right_ref.shape[1]
    block = right_ref.shape[0] // sources
    total = jnp.zeros_like(term_ref)
    for a in range(sources):
        both = received_ref[a, block * cols :].astype(f32)
        total += both[:heads] + both[heads:]
        p = a % inner * (sources // inner) + a // inner
        for k in range(block):
            right_ref[p * block + k] = received_ref[a, k * cols : (k + 1) * cols]
    term_ref[...] = total
    size = pieces[0].shape[0]
    for s, piece in enumerate(pieces):
        left_ref[pl.ds(pl.multiple_of((scalars[0] ^ s) * size, size), size)] = piece[...]


def shards(
    n_seq,
    n_res,
    alignment_query,
    alignment_key,
    attended_vectors,
    attended_cotangent,
    chain_index_per_residue,
    pair,
    pair_bias_matrix,
    left_operand_input,
    right_operand_input,
):
    own, residues, channels = alignment_query.shape
    devices = n_seq * n_res
    spread = 2 - n_seq % 2, 2 - n_res % 2
    groups = spread[0] * spread[1]
    held = HEADS // groups
    width = held * HEAD_DIM
    rows, cols, pair_channels = pair.shape
    block = residues // devices
    a, b = lax.axis_index("seq"), lax.axis_index("res")
    flat = a * n_res + b

    bias = jnp.einsum("ijc,ch->hij", pair, pair_bias_matrix, preferred_element_type=f32)
    bias = bias.reshape(groups, held, rows, cols).transpose(0, 3, 1, 2)
    bias = bias.reshape(1, spread[0], 1, spread[1], cols, held * rows)
    by_group = (n_seq // spread[0], spread[0], n_res // spread[1], spread[1], cols, held * rows)
    bias = jnp.broadcast_to(bias, by_group)
    bias = lax.all_to_all(
        bias.reshape(devices, cols, held * rows), BOTH, 0, 0, tiled=True
    )

    place = a % spread[0] * spread[1] + b % spread[1]
    smem, vmem = [pl.BlockSpec(memory_space=s) for s in (pltpu.SMEM, pltpu.VMEM)]
    params = pltpu.CompilerParams(vmem_limit_bytes=12 * 1024 * 1024)
    hbm = pl.BlockSpec(memory_space=pl.ANY)
    packed = (own, residues, 4 * width)
    right_parts = (n_seq // n_res, n_res, block, cols, pair_channels)
    pieces = pl.pallas_call(
        functools.partial(pack_kernel, groups, n_res),
        in_specs=[smem, vmem] + [hbm] * 6,
        out_shape=[jax.ShapeDtypeStruct((1, residues), jnp.int32)]
        + [jax.ShapeDtypeStruct(packed, bf16)] * groups
        + [jax.ShapeDtypeStruct((2, block, rows, pair_channels), bf16)] * n_res,
        scratch_shapes=[
            pltpu.VMEM((4,) + alignment_query.shape, bf16),
            pltpu.VMEM((groups,) + packed, bf16),
            pltpu.SemaphoreType.DMA((4,)),
            pltpu.SemaphoreType.DMA((n_res * (1 + n_seq // n_res),)),
        ],
        compiler_params=params,
        name="pack",
    )(
        jnp.stack([place, b]).astype(jnp.int32),
        chain_index_per_residue.reshape(1, residues),
        alignment_query,
        alignment_key,
        attended_vectors,
        attended_cotangent,
        left_operand_input,
        right_operand_input.reshape(right_parts),
    )
    chain, arrays, triangles = pieces[0], pieces[1 : 1 + groups], pieces[1 + groups :]

    def peer(x, s):
        pairs = [
            (d, (d // n_res ^ s // spread[1]) * n_res + (d % n_res ^ s % spread[1]))
            for d in range(devices)
        ]
        return lax.ppermute(x, BOTH, pairs)

    def partner(x, s):
        return lax.ppermute(x, "res", [(i, i ^ s) for i in range(n_res)])

    arrays = list(arrays[:1]) + [peer(arrays[s], s) for s in range(1, groups)]

    inner = 2 - n_seq % 2
    half = n_seq // inner
    triangles = list(triangles[:1]) + [partner(triangles[s], s) for s in range(1, n_res)]
    arrays, triangles = lax.optimization_barrier((arrays, triangles))
    left, rights = pl.pallas_call(
        order_kernel,
        in_specs=[smem] + [vmem] * n_res,
        out_shape=[
            jax.ShapeDtypeStruct((block, residues, pair_channels), bf16),
            jax.ShapeDtypeStruct((n_seq, block, cols, pair_channels), bf16),
        ],
        compiler_params=params,
        name="order",
    )(b.reshape(1), *triangles)
    pairs = []
    for d in range(devices):
        g = d // n_res * n_res + turn(d % n_res, n_res)
        p = g % n_seq
        pairs.append((d, (p % half * inner + p // half) * n_res + g // n_seq))
    left = lax.ppermute(left, BOTH, pairs)
    rights = lax.all_to_all(rights, "seq", 0, 0, tiled=True)

    each = max(1, 128 // width)
    slots = (3 * own // each, residues, each * width)
    outs = pl.pallas_call(
        functools.partial(attention_kernel, n_seq, n_res, groups),
        out_shape=[jax.ShapeDtypeStruct(slots, bf16)] * groups
        + [jax.ShapeDtypeStruct(bias.shape, bf16)],
        scratch_shapes=[pltpu.VMEM((held, residues, residues), f32)] * 2,
        compiler_params=params,
        name="attention",
    )(bias, chain, *arrays)
    grads, share = outs[:groups], outs[groups]

    share, rights = lax.optimization_barrier((share, rights))
    share = lax.all_to_all(share, BOTH, 0, 0, tiled=True)
    share, left = lax.optimization_barrier((share, left))
    share = jnp.sum(share.astype(f32).reshape(by_group), axis=(0, 2))
    share = share.reshape(groups, cols, held * rows)
    parity = [list(range(c, devices, 2)) for c in range(2)]
    near = jnp.broadcast_to(share.astype(bf16)[None], (devices // 2,) + share.shape)
    near = lax.all_to_all(near, BOTH, 0, 0, axis_index_groups=parity, tiled=True)
    own_grad = share.reshape(groups, cols, held, rows).transpose(0, 2, 3, 1)
    own_grad = own_grad.reshape(HEADS, rows, cols)
    term = jnp.einsum(
        "ijc,hij->hc", pair.astype(f32), own_grad, precision=lax.Precision.HIGHEST
    )
    term = sum([term] + [partner(term, s) for s in range(1, n_res)])
    rights = [rights, partner(rights, 1)]
    extra = jnp.stack([pair_bias_matrix.astype(f32).T, term])
    near, extra, rights = lax.optimization_barrier((near, extra, rights))
    far = partner(near, 1)

    across = n_res // 2
    d_right = pl.pallas_call(
        functools.partial(d_right_kernel, n_seq, n_res),
        in_specs=[smem] + [vmem] * 4,
        out_shape=jax.ShapeDtypeStruct((n_seq, block * cols + 2 * HEADS, pair_channels), bf16),
        scratch_shapes=[
            pltpu.VMEM((HEADS, residues, residues), bf16),
        ],
        compiler_params=params,
        name="d_right",
    )((b % 2).reshape(1), near, far, extra, left)
    d_right = lax.all_to_all(d_right, "seq", 0, 0, tiled=True)

    piece = (2 * block, rows, pair_channels)
    d_left = pl.pallas_call(
        functools.partial(d_left_kernel, n_seq, n_res),
        in_specs=[smem] + [vmem] * 4,
        out_shape=[jax.ShapeDtypeStruct(piece, bf16)] * across,
        scratch_shapes=[
            pltpu.VMEM((across,) + piece, bf16),
            pltpu.VMEM((HEADS, across * rows, residues), bf16),
            pltpu.VMEM((2, block, residues, pair_channels), bf16),
        ],
        compiler_params=params,
        name="d_left",
    )(jnp.stack([b % 2, b // 2]).astype(jnp.int32), near, extra, *rights)
    d_left = list(d_left[:1]) + [partner(d_left[s], 2 * s) for s in range(1, across)]
    grads = [grads[0]] + [peer(grads[s], s) for s in range(1, groups)]
    d_left, grads = lax.optimization_barrier((d_left, grads))
    query_gradient, key_gradient, value_gradient = pl.pallas_call(
        unpack_kernel,
        in_specs=[smem] + [vmem] * groups,
        out_shape=[jax.ShapeDtypeStruct(alignment_query.shape, bf16)] * 3,
        scratch_shapes=[pltpu.VMEM((groups,) + slots, bf16)],
        compiler_params=params,
        name="unpack",
    )(place.reshape(1), *grads)

    d_bias_weight, d_left, d_right = pl.pallas_call(
        functools.partial(place_kernel, inner),
        in_specs=[smem] + [vmem] * (1 + across),
        out_shape=[
            jax.ShapeDtypeStruct((HEADS, pair_channels), f32),
            jax.ShapeDtypeStruct((across * 2 * block, rows, pair_channels), bf16),
            jax.ShapeDtypeStruct((n_seq * block, cols, pair_channels), bf16),
        ],
        compiler_params=params,
        name="place",
    )((b // 2).reshape(1), d_right, *d_left)
    d_bias_weight = d_bias_weight.T
    return (query_gradient, key_gradient, value_gradient, d_bias_weight, d_left, d_right)


def solution(mesh):
    placed = (
        P(BOTH, None, None),
        P(BOTH, None, None),
        P(BOTH, None, None),
        P(BOTH, None, None),
        P(),
        P("res", "seq", None),
        P(),
        P("seq", "res", None),
        P("res", "seq", None),
    )
    return jax.shard_map(
        functools.partial(shards, mesh.shape["seq"], mesh.shape["res"]),
        mesh=mesh,
        in_specs=placed,
        out_specs=(
            P(BOTH, None, None),
            P(BOTH, None, None),
            P(BOTH, None, None),
            P(),
            P("seq", "res", None),
            P("res", "seq", None),
        ),
        check_vma=False,
    )
```

```python
import functools
import math

import jax
import jax.numpy as jnp
from jax import lax
from jax.experimental import pallas as pl
from jax.experimental.pallas import tpu as pltpu
from jax.sharding import PartitionSpec as P

HEADS = 8
HEAD_DIM = 32
BIG_NEGATIVE = -1e30
BOTH = ("seq", "res")
NT = (((1,), (1,)), ((), ()))
TN = (((0,), (0,)), ((), ()))

f32 = jnp.float32
bf16 = jnp.bfloat16


def attention_kernel(
    n_seq, n_res, groups, bias_ref, chain_ref, *refs
):
    arrays, grads = refs[:groups], refs[groups : 2 * groups]
    share_ref, masked, total = refs[2 * groups :]
    heads, residues, _ = masked.shape
    cols, rows = residues // n_seq, residues // n_res
    width = heads * HEAD_DIM
    scale = HEAD_DIM**-0.5

    chain_row = chain_ref[...].astype(f32)
    chain_col = jnp.broadcast_to(chain_row, (8, residues)).T[:, :1]
    for h in range(heads):
        for a in range(n_seq):
            band = jnp.concatenate(
                [bias_ref[a * n_res + b, :, h * rows : (h + 1) * rows] for b in range(n_res)],
                axis=-1,
            )
            allowed = chain_col[a * cols : (a + 1) * cols] == chain_row
            masked[h, a * cols : (a + 1) * cols, :] = jnp.where(allowed, band, BIG_NEGATIVE)
    total[...] = jnp.zeros_like(total)

    def sequence(x_ref, n):
        query_parts, key_parts, value_parts = [], [], []
        for h in range(heads):
            q, k, v, g = [
                x_ref[n, :, t * width + h * HEAD_DIM : t * width + (h + 1) * HEAD_DIM]
                for t in range(4)
            ]
            scores = lax.dot_general(k, q, NT, preferred_element_type=f32) * scale + masked[h]
            top = jnp.max(scores, axis=0, keepdims=True)
            expo = jnp.exp(scores - top)
            probs = expo * (1.0 / jnp.sum(expo, axis=0, keepdims=True))
            dprobs = lax.dot_general(v, g, NT, preferred_element_type=f32)
            dscores = probs * (dprobs - jnp.sum(probs * dprobs, axis=0, keepdims=True))
            total[h] += dscores
            dscores_b = dscores.astype(bf16)
            query_parts.append(
                lax.dot_general(dscores_b, k, TN, preferred_element_type=f32) * scale
            )
            key_parts.append(jnp.dot(dscores_b, q, preferred_element_type=f32) * scale)
            value_parts.append(jnp.dot(probs.astype(bf16), g, preferred_element_type=f32))
        return [
            jnp.concatenate(parts, axis=-1).astype(bf16)
            for parts in (query_parts, key_parts, value_parts)
        ]

    for s in range(groups):
        units = sum([sequence(arrays[s], n) for n in range(arrays[s].shape[0])], [])
        slots = grads[s].shape[0]
        each = len(units) // slots
        for n in range(slots):
            grads[s][n] = jnp.concatenate(units[n * each : (n + 1) * each], axis=-1)

    for a in range(n_seq):
        for b in range(n_res):
            share_ref[a * n_res + b] = jnp.concatenate(
                [
                    total[h, a * cols : (a + 1) * cols, b * rows : (b + 1) * rows]
                    for h in range(heads)
                ],
                axis=-1,
            ).astype(bf16)


def unpack_kernel(place_ref, *refs):
    pieces, outs, held = refs[:-4], refs[-4:-1], refs[-1]
    groups = len(pieces)
    own = outs[0].shape[0]
    slots, _, lanes = pieces[0].shape
    each = 3 * own // slots
    width = lanes // each
    for s in range(groups):
        held[s] = pieces[s][...]
    place = place_ref[0]
    for t in range(3):
        for n in range(own):
            slot, start = (3 * n + t) // each, (3 * n + t) % each * width
            outs[t][n] = jnp.concatenate(
                [held[place ^ g, slot, :, start : start + width] for g in range(groups)], axis=-1
            )


def pack_kernel(groups, n_res, scalars, chain_ref, *refs):
    arrays, (left_ref, right_ref), refs = refs[:4], refs[4:6], refs[6:]
    chain_out, outs, triangles = refs[0], refs[1 : 1 + groups], refs[1 + groups : -4]
    whole, held, loaded, sent = refs[-4:]
    place, b = scalars[0], scalars[1]
    block, rows = triangles[0].shape[1:3]
    cols = right_ref.shape[-2]
    loads = [
        pltpu.make_async_copy(x, whole.at[n], loaded.at[n]) for n, x in enumerate(arrays)
    ]
    for load in loads:
        load.start()
    copies = []
    for s in range(n_res):
        t = turn(b ^ s, n_res) * block
        copies.append((left_ref.at[pl.ds(t, block)], triangles[s].at[0]))
        for y in range(rows // cols):
            copies.append(
                (right_ref.at[y, b ^ s], triangles[s].at[1, :, y * cols : (y + 1) * cols])
            )
    copies = [pltpu.make_async_copy(x, y, sent.at[n]) for n, (x, y) in enumerate(copies)]
    for copy in copies:
        copy.start()
    chain_out[...] = chain_ref[...]
    for load in loads:
        load.wait()
    width = whole.shape[-1] // groups
    for g in range(groups):
        held[g] = jnp.concatenate(
            [whole[n, :, :, g * width : (g + 1) * width] for n in range(4)], axis=-1
        )
    for s in range(groups):
        outs[s][...] = held[place ^ s]
    for copy in copies:
        copy.wait()


def turn(b, n_res):
    return b % 2 * (n_res // 2) + b // 2


def order_kernel(scalars, *refs):
    pieces, (left_ref, chunks_ref) = refs[:-2], refs[-2:]
    rows, cols = pieces[0].shape[2], chunks_ref.shape[2]
    each = rows // cols
    for s, piece in enumerate(pieces):
        b = scalars[0] ^ s
        left_ref[:, pl.ds(pl.multiple_of(b * rows, rows), rows), :] = piece[0]
        for y in range(each):
            chunks_ref[b * each + y] = piece[1, :, y * cols : (y + 1) * cols]


def pairs_of(block):
    return [(k, min(2, block - k)) for k in range(0, block, 2)]


def d_left_kernel(n_seq, n_res, scalars, near_ref, extra_ref, *refs):
    rights, outs = refs[:2], refs[2:-2]
    flat, right = refs[-2:]
    heads, count, residues = flat.shape
    held = heads // near_ref.shape[1]
    cols, rows = residues // n_seq, residues // n_res
    across = n_res // 2
    block = rights[0].shape[1]
    core, x = scalars[0], scalars[1]
    for part in range(2):
        where = core ^ part
        for a in range(n_seq):
            right[where, :, a * cols : (a + 1) * cols, :] = rights[part][a]
    for h in range(heads):
        group, place = h // held, h % held
        turned = jnp.concatenate(
            [
                jnp.concatenate(
                    [
                        near_ref[a * across + u, group, :, place * rows : (place + 1) * rows]
                        for u in range(across)
                    ],
                    axis=-1,
                )
                for a in range(n_seq)
            ],
            axis=0,
        )
        flat[h] = turned.astype(f32).T.astype(bf16)
    sums = outs[-1]
    channels = right.shape[-1]
    for c in range(2):
        for k, wide in pairs_of(block):
            both = jnp.concatenate([right[c, k + n] for n in range(wide)], axis=-1)
            row = jnp.zeros((count, wide * channels), f32)
            for h in range(heads):
                weight = jnp.concatenate([extra_ref[0, h : h + 1, :]] * wide, axis=-1)
                row += jnp.dot(flat[h], both, preferred_element_type=f32) * weight
            for n in range(wide):
                part = row[:, n * channels : (n + 1) * channels].astype(bf16)
                for u in range(across):
                    sums[u, c * block + k + n] = part[u * rows : (u + 1) * rows]
    for s in range(across):
        outs[s][...] = sums[x ^ s]


def d_right_kernel(n_seq, n_res, scalars, near_ref, far_ref, extra_ref, left, out, turned):
    heads, residues, _ = turned.shape
    held = heads // near_ref.shape[1]
    cols, rows = residues // n_seq, residues // n_res
    across = n_res // 2
    block = left.shape[0]
    core = scalars[0]
    for h in range(heads):
        group, place = h // held, h % held
        for a in range(n_seq):
            band = []
            for b in range(n_res):
                piece = (
                    a * across + b // 2, group, slice(None), slice(place * rows, (place + 1) * rows)
                )
                band.append(jnp.where(core == b % 2, near_ref[piece], far_ref[piece]))
            turned[h, a * cols : (a + 1) * cols, :] = jnp.concatenate(band, axis=-1)
    channels = left.shape[-1]
    for k, wide in pairs_of(block):
        both = jnp.concatenate([left[k + n] for n in range(wide)], axis=-1)
        row = jnp.zeros((residues, wide * channels), f32)
        for h in range(heads):
            weight = jnp.concatenate([extra_ref[0, h : h + 1, :]] * wide, axis=-1)
            row += jnp.dot(turned[h], both, preferred_element_type=f32) * weight
        for n in range(wide):
            part = row[:, n * channels : (n + 1) * channels].astype(bf16)
            for a in range(n_seq):
                out[a, (k + n) * cols : (k + n + 1) * cols] = part[a * cols : (a + 1) * cols]
    term = extra_ref[1]
    high = term.astype(bf16).astype(f32)
    both = jnp.concatenate([high, term - high], axis=0).astype(bf16)
    for a in range(n_seq):
        out[a, block * cols :] = both


def place_kernel(inner, scalars, received_ref, *refs):
    pieces, (term_ref, left_ref, right_ref) = refs[:-3], refs[-3:]
    heads = term_ref.shape[0]
    sources, size, _ = received_ref.shape
    cols = right_ref.shape[1]
    block = right_ref.shape[0] // sources
    total = jnp.zeros_like(term_ref)
    for a in range(sources):
        both = received_ref[a, block * cols :].astype(f32)
        total += both[:heads] + both[heads:]
        p = a % inner * (sources // inner) + a // inner
        for k in range(block):
            right_ref[p * block + k] = received_ref[a, k * cols : (k + 1) * cols]
    term_ref[...] = total
    size = pieces[0].shape[0]
    for s, piece in enumerate(pieces):
        left_ref[pl.ds(pl.multiple_of((scalars[0] ^ s) * size, size), size)] = piece[...]


def shards(
    n_seq,
    n_res,
    alignment_query,
    alignment_key,
    attended_vectors,
    attended_cotangent,
    chain_index_per_residue,
    pair,
    pair_bias_matrix,
    left_operand_input,
    right_operand_input,
):
    own, residues, channels = alignment_query.shape
    devices = n_seq * n_res
    spread = 2 - n_seq % 2, 2 - n_res % 2
    groups = spread[0] * spread[1]
    held = HEADS // groups
    width = held * HEAD_DIM
    rows, cols, pair_channels = pair.shape
    block = residues // devices
    a, b = lax.axis_index("seq"), lax.axis_index("res")
    flat = a * n_res + b

    bias = jnp.einsum("ijc,ch->hij", pair, pair_bias_matrix, preferred_element_type=f32)
    bias = bias.reshape(groups, held, rows, cols).transpose(0, 3, 1, 2)
    bias = bias.reshape(1, spread[0], 1, spread[1], cols, held * rows)
    by_group = (n_seq // spread[0], spread[0], n_res // spread[1], spread[1], cols, held * rows)
    bias = jnp.broadcast_to(bias, by_group)
    bias = lax.all_to_all(
        bias.reshape(devices, cols, held * rows), BOTH, 0, 0, tiled=True
    )

    place = a % spread[0] * spread[1] + b % spread[1]
    smem, vmem = [pl.BlockSpec(memory_space=s) for s in (pltpu.SMEM, pltpu.VMEM)]
    params = pltpu.CompilerParams(vmem_limit_bytes=12 * 1024 * 1024)
    hbm = pl.BlockSpec(memory_space=pl.ANY)
    packed = (own, residues, 4 * width)
    right_parts = (n_seq // n_res, n_res, block, cols, pair_channels)
    pieces = pl.pallas_call(
        functools.partial(pack_kernel, groups, n_res),
        in_specs=[smem, vmem] + [hbm] * 6,
        out_shape=[jax.ShapeDtypeStruct((1, residues), jnp.int32)]
        + [jax.ShapeDtypeStruct(packed, bf16)] * groups
        + [jax.ShapeDtypeStruct((2, block, rows, pair_channels), bf16)] * n_res,
        scratch_shapes=[
            pltpu.VMEM((4,) + alignment_query.shape, bf16),
            pltpu.VMEM((groups,) + packed, bf16),
            pltpu.SemaphoreType.DMA((4,)),
            pltpu.SemaphoreType.DMA((n_res * (1 + n_seq // n_res),)),
        ],
        compiler_params=params,
        name="pack",
    )(
        jnp.stack([place, b]).astype(jnp.int32),
        chain_index_per_residue.reshape(1, residues),
        alignment_query,
        alignment_key,
        attended_vectors,
        attended_cotangent,
        left_operand_input,
        right_operand_input.reshape(right_parts),
    )
    chain, arrays, triangles = pieces[0], pieces[1 : 1 + groups], pieces[1 + groups :]

    def peer(x, s):
        pairs = [
            (d, (d // n_res ^ s // spread[1]) * n_res + (d % n_res ^ s % spread[1]))
            for d in range(devices)
        ]
        return lax.ppermute(x, BOTH, pairs)

    def partner(x, s):
        return lax.ppermute(x, "res", [(i, i ^ s) for i in range(n_res)])

    arrays = list(arrays[:1]) + [peer(arrays[s], s) for s in range(1, groups)]

    inner = 2 - n_seq % 2
    half = n_seq // inner
    triangles = list(triangles[:1]) + [partner(triangles[s], s) for s in range(1, n_res)]
    arrays, triangles = lax.optimization_barrier((arrays, triangles))
    left, rights = pl.pallas_call(
        order_kernel,
        in_specs=[smem] + [vmem] * n_res,
        out_shape=[
            jax.ShapeDtypeStruct((block, residues, pair_channels), bf16),
            jax.ShapeDtypeStruct((n_seq, block, cols, pair_channels), bf16),
        ],
        compiler_params=params,
        name="order",
    )(b.reshape(1), *triangles)
    pairs = []
    for d in range(devices):
        g = d // n_res * n_res + turn(d % n_res, n_res)
        p = g % n_seq
        pairs.append((d, (p % half * inner + p // half) * n_res + g // n_seq))
    left = lax.ppermute(left, BOTH, pairs)
    rights = lax.all_to_all(rights, "seq", 0, 0, tiled=True)

    each = max(1, 128 // width)
    slots = (3 * own // each, residues, each * width)
    outs = pl.pallas_call(
        functools.partial(attention_kernel, n_seq, n_res, groups),
        out_shape=[jax.ShapeDtypeStruct(slots, bf16)] * groups
        + [jax.ShapeDtypeStruct(bias.shape, bf16)],
        scratch_shapes=[pltpu.VMEM((held, residues, residues), f32)] * 2,
        compiler_params=params,
        name="attention",
    )(bias, chain, *arrays)
    grads, share = outs[:groups], outs[groups]

    share, rights = lax.optimization_barrier((share, rights))
    share = lax.all_to_all(share, BOTH, 0, 0, tiled=True)
    share, left = lax.optimization_barrier((share, left))
    share = jnp.sum(share.astype(f32).reshape(by_group), axis=(0, 2))
    share = share.reshape(groups, cols, held * rows)
    parity = [list(range(c, devices, 2)) for c in range(2)]
    near = jnp.broadcast_to(share.astype(bf16)[None], (devices // 2,) + share.shape)
    near = lax.all_to_all(near, BOTH, 0, 0, axis_index_groups=parity, tiled=True)
    own_grad = share.reshape(groups, cols, held, rows).transpose(0, 2, 3, 1)
    own_grad = own_grad.reshape(HEADS, rows, cols)
    term = jnp.einsum(
        "ijc,hij->hc", pair.astype(f32), own_grad, precision=lax.Precision.HIGHEST
    )
    term = sum([term] + [partner(term, s) for s in range(1, n_res)])
    rights = [rights, partner(rights, 1)]
    extra = jnp.stack([pair_bias_matrix.astype(f32).T, term])
    grads = list(grads)
    for s in (1, 3):
        grads[s] = peer(grads[s], s)
    early = [grads[s] for s in (1, 3)]
    near, extra, rights, early = lax.optimization_barrier((near, extra, rights, early))
    for s, piece in zip((1, 3), early):
        grads[s] = piece
    far = partner(near, 1)

    across = n_res // 2
    d_right = pl.pallas_call(
        functools.partial(d_right_kernel, n_seq, n_res),
        in_specs=[smem] + [vmem] * 4,
        out_shape=jax.ShapeDtypeStruct((n_seq, block * cols + 2 * HEADS, pair_channels), bf16),
        scratch_shapes=[
            pltpu.VMEM((HEADS, residues, residues), bf16),
        ],
        compiler_params=params,
        name="d_right",
    )((b % 2).reshape(1), near, far, extra, left)
    d_right = lax.all_to_all(d_right, "seq", 0, 0, tiled=True)

    piece = (2 * block, rows, pair_channels)
    d_left = pl.pallas_call(
        functools.partial(d_left_kernel, n_seq, n_res),
        in_specs=[smem] + [vmem] * 4,
        out_shape=[jax.ShapeDtypeStruct(piece, bf16)] * across,
        scratch_shapes=[
            pltpu.VMEM((across,) + piece, bf16),
            pltpu.VMEM((HEADS, across * rows, residues), bf16),
            pltpu.VMEM((2, block, residues, pair_channels), bf16),
        ],
        compiler_params=params,
        name="d_left",
    )(jnp.stack([b % 2, b // 2]).astype(jnp.int32), near, extra, *rights)
    d_left = list(d_left[:1]) + [partner(d_left[s], 2 * s) for s in range(1, across)]
    for s in range(1, groups):
        if s not in (1, 3):
            grads[s] = peer(grads[s], s)
    d_left, grads = lax.optimization_barrier((d_left, grads))
    query_gradient, key_gradient, value_gradient = pl.pallas_call(
        unpack_kernel,
        in_specs=[smem] + [vmem] * groups,
        out_shape=[jax.ShapeDtypeStruct(alignment_query.shape, bf16)] * 3,
        scratch_shapes=[pltpu.VMEM((groups,) + slots, bf16)],
        compiler_params=params,
        name="unpack",
    )(place.reshape(1), *grads)

    d_bias_weight, d_left, d_right = pl.pallas_call(
        functools.partial(place_kernel, inner),
        in_specs=[smem] + [vmem] * (1 + across),
        out_shape=[
            jax.ShapeDtypeStruct((HEADS, pair_channels), f32),
            jax.ShapeDtypeStruct((across * 2 * block, rows, pair_channels), bf16),
            jax.ShapeDtypeStruct((n_seq * block, cols, pair_channels), bf16),
        ],
        compiler_params=params,
        name="place",
    )((b // 2).reshape(1), d_right, *d_left)
    d_bias_weight = d_bias_weight.T
    return (query_gradient, key_gradient, value_gradient, d_bias_weight, d_left, d_right)


def solution(mesh):
    placed = (
        P(BOTH, None, None),
        P(BOTH, None, None),
        P(BOTH, None, None),
        P(BOTH, None, None),
        P(),
        P("res", "seq", None),
        P(),
        P("seq", "res", None),
        P("res", "seq", None),
    )
    return jax.shard_map(
        functools.partial(shards, mesh.shape["seq"], mesh.shape["res"]),
        mesh=mesh,
        in_specs=placed,
        out_specs=(
            P(BOTH, None, None),
            P(BOTH, None, None),
            P(BOTH, None, None),
            P(),
            P("seq", "res", None),
            P("res", "seq", None),
        ),
        check_vma=False,
    )
```

```python
import functools
import math

import jax
import jax.numpy as jnp
from jax import lax
from jax.experimental import pallas as pl
from jax.experimental.pallas import tpu as pltpu
from jax.sharding import PartitionSpec as P

HEADS = 8
HEAD_DIM = 32
BIG_NEGATIVE = -1e30
BOTH = ("seq", "res")
NT = (((1,), (1,)), ((), ()))
TN = (((0,), (0,)), ((), ()))

f32 = jnp.float32
bf16 = jnp.bfloat16


def attention_kernel(
    n_seq, n_res, groups, bias_ref, chain_ref, *refs
):
    arrays, grads = refs[:groups], refs[groups : 2 * groups]
    share_ref, masked, total = refs[2 * groups :]
    heads, residues, _ = masked.shape
    cols, rows = residues // n_seq, residues // n_res
    width = heads * HEAD_DIM
    scale = HEAD_DIM**-0.5

    chain_row = chain_ref[...].astype(f32)
    chain_col = jnp.broadcast_to(chain_row, (8, residues)).T[:, :1]
    for h in range(heads):
        for a in range(n_seq):
            band = jnp.concatenate(
                [bias_ref[a * n_res + b, :, h * rows : (h + 1) * rows] for b in range(n_res)],
                axis=-1,
            )
            allowed = chain_col[a * cols : (a + 1) * cols] == chain_row
            masked[h, a * cols : (a + 1) * cols, :] = jnp.where(allowed, band, BIG_NEGATIVE)
    total[...] = jnp.zeros_like(total)

    def sequence(x_ref, n):
        query_parts, key_parts, value_parts = [], [], []
        for h in range(heads):
            q, k, v, g = [
                x_ref[n, :, t * width + h * HEAD_DIM : t * width + (h + 1) * HEAD_DIM]
                for t in range(4)
            ]
            scores = lax.dot_general(k, q, NT, preferred_element_type=f32) * scale + masked[h]
            top = jnp.max(scores, axis=0, keepdims=True)
            expo = jnp.exp(scores - top)
            probs = expo * (1.0 / jnp.sum(expo, axis=0, keepdims=True))
            dprobs = lax.dot_general(v, g, NT, preferred_element_type=f32)
            dscores = probs * (dprobs - jnp.sum(probs * dprobs, axis=0, keepdims=True))
            total[h] += dscores
            dscores_b = dscores.astype(bf16)
            query_parts.append(
                lax.dot_general(dscores_b, k, TN, preferred_element_type=f32) * scale
            )
            key_parts.append(jnp.dot(dscores_b, q, preferred_element_type=f32) * scale)
            value_parts.append(jnp.dot(probs.astype(bf16), g, preferred_element_type=f32))
        return [
            jnp.concatenate(parts, axis=-1).astype(bf16)
            for parts in (query_parts, key_parts, value_parts)
        ]

    for s in range(groups):
        units = sum([sequence(arrays[s], n) for n in range(arrays[s].shape[0])], [])
        slots = grads[s].shape[0]
        each = len(units) // slots
        for n in range(slots):
            grads[s][n] = jnp.concatenate(units[n * each : (n + 1) * each], axis=-1)

    for a in range(n_seq):
        for b in range(n_res):
            share_ref[a * n_res + b] = jnp.concatenate(
                [
                    total[h, a * cols : (a + 1) * cols, b * rows : (b + 1) * rows]
                    for h in range(heads)
                ],
                axis=-1,
            ).astype(bf16)


def unpack_kernel(place_ref, *refs):
    pieces, outs, held = refs[:-4], refs[-4:-1], refs[-1]
    groups = len(pieces)
    own = outs[0].shape[0]
    slots, _, lanes = pieces[0].shape
    each = 3 * own // slots
    width = lanes // each
    for s in range(groups):
        held[s] = pieces[s][...]
    place = place_ref[0]
    for t in range(3):
        for n in range(own):
            slot, start = (3 * n + t) // each, (3 * n + t) % each * width
            outs[t][n] = jnp.concatenate(
                [held[place ^ g, slot, :, start : start + width] for g in range(groups)], axis=-1
            )


def pack_kernel(groups, n_res, scalars, chain_ref, *refs):
    arrays, (left_ref, right_ref), refs = refs[:4], refs[4:6], refs[6:]
    chain_out, outs, triangles, held = refs[0], refs[1 : 1 + groups], refs[1 + groups : -1], refs[-1]
    place, b = scalars[0], scalars[1]
    block, rows = triangles[0].shape[1:3]
    cols = right_ref.shape[-2]
    width = held.shape[-1] // 4
    for g in range(groups):
        held[g] = jnp.concatenate(
            [x[:, :, g * width : (g + 1) * width] for x in arrays], axis=-1
        )
    for s in range(groups):
        outs[s][...] = held[place ^ s]
    for s in range(n_res):
        t = turn(b ^ s, n_res) * block
        triangles[s][0] = left_ref[pl.ds(t, block)]
        for y in range(rows // cols):
            triangles[s][1, :, y * cols : (y + 1) * cols] = right_ref[y, b ^ s]
    chain_out[...] = chain_ref[...]


def turn(b, n_res):
    return b % 2 * (n_res // 2) + b // 2


def order_kernel(scalars, *refs):
    pieces, (left_ref, chunks_ref) = refs[:-2], refs[-2:]
    rows, cols = pieces[0].shape[2], chunks_ref.shape[2]
    each = rows // cols
    for s, piece in enumerate(pieces):
        b = scalars[0] ^ s
        left_ref[:, pl.ds(pl.multiple_of(b * rows, rows), rows), :] = piece[0]
        for y in range(each):
            chunks_ref[b * each + y] = piece[1, :, y * cols : (y + 1) * cols]


def pairs_of(block):
    return [(k, min(2, block - k)) for k in range(0, block, 2)]


def d_left_kernel(n_seq, n_res, scalars, near_ref, extra_ref, *refs):
    rights, outs = refs[:2], refs[2:-2]
    flat, right = refs[-2:]
    heads, count, residues = flat.shape
    held = heads // near_ref.shape[1]
    cols, rows = residues // n_seq, residues // n_res
    across = n_res // 2
    block = rights[0].shape[1]
    core, x = scalars[0], scalars[1]
    for part in range(2):
        where = core ^ part
        for a in range(n_seq):
            right[where, :, a * cols : (a + 1) * cols, :] = rights[part][a]
    for h in range(heads):
        group, place = h // held, h % held
        turned = jnp.concatenate(
            [
                jnp.concatenate(
                    [
                        near_ref[a * across + u, group, :, place * rows : (place + 1) * rows]
                        for u in range(across)
                    ],
                    axis=-1,
                )
                for a in range(n_seq)
            ],
            axis=0,
        )
        flat[h] = turned.astype(f32).T.astype(bf16)
    sums = outs[-1]
    channels = right.shape[-1]
    for c in range(2):
        for k, wide in pairs_of(block):
            both = jnp.concatenate([right[c, k + n] for n in range(wide)], axis=-1)
            row = jnp.zeros((count, wide * channels), f32)
            for h in range(heads):
                weight = jnp.concatenate([extra_ref[0, h : h + 1, :]] * wide, axis=-1)
                row += jnp.dot(flat[h], both, preferred_element_type=f32) * weight
            for n in range(wide):
                part = row[:, n * channels : (n + 1) * channels].astype(bf16)
                for u in range(across):
                    sums[u, c * block + k + n] = part[u * rows : (u + 1) * rows]
    for s in range(across):
        outs[s][...] = sums[x ^ s]


def d_right_kernel(n_seq, n_res, scalars, near_ref, far_ref, extra_ref, left, out, turned):
    heads, residues, _ = turned.shape
    held = heads // near_ref.shape[1]
    cols, rows = residues // n_seq, residues // n_res
    across = n_res // 2
    block = left.shape[0]
    core = scalars[0]
    for h in range(heads):
        group, place = h // held, h % held
        for a in range(n_seq):
            band = []
            for b in range(n_res):
                piece = (
                    a * across + b // 2, group, slice(None), slice(place * rows, (place + 1) * rows)
                )
                band.append(jnp.where(core == b % 2, near_ref[piece], far_ref[piece]))
            turned[h, a * cols : (a + 1) * cols, :] = jnp.concatenate(band, axis=-1)
    channels = left.shape[-1]
    for k, wide in pairs_of(block):
        both = jnp.concatenate([left[k + n] for n in range(wide)], axis=-1)
        row = jnp.zeros((residues, wide * channels), f32)
        for h in range(heads):
            weight = jnp.concatenate([extra_ref[0, h : h + 1, :]] * wide, axis=-1)
            row += jnp.dot(turned[h], both, preferred_element_type=f32) * weight
        for n in range(wide):
            part = row[:, n * channels : (n + 1) * channels].astype(bf16)
            for a in range(n_seq):
                out[a, (k + n) * cols : (k + n + 1) * cols] = part[a * cols : (a + 1) * cols]
    term = extra_ref[1]
    high = term.astype(bf16).astype(f32)
    both = jnp.concatenate([high, term - high], axis=0).astype(bf16)
    for a in range(n_seq):
        out[a, block * cols :] = both


def place_kernel(inner, scalars, received_ref, *refs):
    pieces, (term_ref, left_ref, right_ref) = refs[:-3], refs[-3:]
    heads = term_ref.shape[0]
    sources, size, _ = received_ref.shape
    cols = right_ref.shape[1]
    block = right_ref.shape[0] // sources
    total = jnp.zeros_like(term_ref)
    for a in range(sources):
        both = received_ref[a, block * cols :].astype(f32)
        total += both[:heads] + both[heads:]
        p = a % inner * (sources // inner) + a // inner
        for k in range(block):
            right_ref[p * block + k] = received_ref[a, k * cols : (k + 1) * cols]
    term_ref[...] = total
    size = pieces[0].shape[0]
    for s, piece in enumerate(pieces):
        left_ref[pl.ds(pl.multiple_of((scalars[0] ^ s) * size, size), size)] = piece[...]


def shards(
    n_seq,
    n_res,
    alignment_query,
    alignment_key,
    attended_vectors,
    attended_cotangent,
    chain_index_per_residue,
    pair,
    pair_bias_matrix,
    left_operand_input,
    right_operand_input,
):
    own, residues, channels = alignment_query.shape
    devices = n_seq * n_res
    spread = 2 - n_seq % 2, 2 - n_res % 2
    groups = spread[0] * spread[1]
    held = HEADS // groups
    width = held * HEAD_DIM
    rows, cols, pair_channels = pair.shape
    block = residues // devices
    a, b = lax.axis_index("seq"), lax.axis_index("res")
    flat = a * n_res + b

    bias = jnp.einsum("ijc,ch->hij", pair, pair_bias_matrix, preferred_element_type=f32)
    bias = bias.reshape(groups, held, rows, cols).transpose(0, 3, 1, 2)
    bias = bias.reshape(1, spread[0], 1, spread[1], cols, held * rows)
    by_group = (n_seq // spread[0], spread[0], n_res // spread[1], spread[1], cols, held * rows)
    bias = jnp.broadcast_to(bias, by_group)
    bias = lax.all_to_all(
        bias.reshape(devices, cols, held * rows), BOTH, 0, 0, tiled=True
    )

    place = a % spread[0] * spread[1] + b % spread[1]
    smem, vmem = [pl.BlockSpec(memory_space=s) for s in (pltpu.SMEM, pltpu.VMEM)]
    params = pltpu.CompilerParams(vmem_limit_bytes=12 * 1024 * 1024)
    packed = (own, residues, 4 * width)
    right_parts = (n_seq // n_res, n_res, block, cols, pair_channels)
    pieces = pl.pallas_call(
        functools.partial(pack_kernel, groups, n_res),
        in_specs=[smem] + [vmem] * 7,
        out_shape=[jax.ShapeDtypeStruct((1, residues), jnp.int32)]
        + [jax.ShapeDtypeStruct(packed, bf16)] * groups
        + [jax.ShapeDtypeStruct((2, block, rows, pair_channels), bf16)] * n_res,
        scratch_shapes=[
            pltpu.VMEM((groups,) + packed, bf16),
        ],
        compiler_params=params,
        name="pack",
    )(
        jnp.stack([place, b]).astype(jnp.int32),
        chain_index_per_residue.reshape(1, residues),
        alignment_query,
        alignment_key,
        attended_vectors,
        attended_cotangent,
        left_operand_input,
        right_operand_input.reshape(right_parts),
    )
    chain, arrays, triangles = pieces[0], pieces[1 : 1 + groups], pieces[1 + groups :]

    def peer(x, s):
        pairs = [
            (d, (d // n_res ^ s // spread[1]) * n_res + (d % n_res ^ s % spread[1]))
            for d in range(devices)
        ]
        return lax.ppermute(x, BOTH, pairs)

    def partner(x, s):
        return lax.ppermute(x, "res", [(i, i ^ s) for i in range(n_res)])

    arrays = list(arrays[:1]) + [peer(arrays[s], s) for s in range(1, groups)]

    inner = 2 - n_seq % 2
    half = n_seq // inner
    triangles = list(triangles[:1]) + [partner(triangles[s], s) for s in range(1, n_res)]
    arrays, triangles = lax.optimization_barrier((arrays, triangles))
    left, rights = pl.pallas_call(
        order_kernel,
        in_specs=[smem] + [vmem] * n_res,
        out_shape=[
            jax.ShapeDtypeStruct((block, residues, pair_channels), bf16),
            jax.ShapeDtypeStruct((n_seq, block, cols, pair_channels), bf16),
        ],
        compiler_params=params,
        name="order",
    )(b.reshape(1), *triangles)
    pairs = []
    for d in range(devices):
        g = d // n_res * n_res + turn(d % n_res, n_res)
        p = g % n_seq
        pairs.append((d, (p % half * inner + p // half) * n_res + g // n_seq))
    left = lax.ppermute(left, BOTH, pairs)
    rights = lax.all_to_all(rights, "seq", 0, 0, tiled=True)

    each = max(1, 128 // width)
    slots = (3 * own // each, residues, each * width)
    outs = pl.pallas_call(
        functools.partial(attention_kernel, n_seq, n_res, groups),
        out_shape=[jax.ShapeDtypeStruct(slots, bf16)] * groups
        + [jax.ShapeDtypeStruct(bias.shape, bf16)],
        scratch_shapes=[pltpu.VMEM((held, residues, residues), f32)] * 2,
        compiler_params=params,
        name="attention",
    )(bias, chain, *arrays)
    grads, share = outs[:groups], outs[groups]

    share, rights = lax.optimization_barrier((share, rights))
    share = lax.all_to_all(share, BOTH, 0, 0, tiled=True)
    share, left = lax.optimization_barrier((share, left))
    share = jnp.sum(share.astype(f32).reshape(by_group), axis=(0, 2))
    share = share.reshape(groups, cols, held * rows)
    parity = [list(range(c, devices, 2)) for c in range(2)]
    near = jnp.broadcast_to(share.astype(bf16)[None], (devices // 2,) + share.shape)
    near = lax.all_to_all(near, BOTH, 0, 0, axis_index_groups=parity, tiled=True)
    own_grad = share.reshape(groups, cols, held, rows).transpose(0, 2, 3, 1)
    own_grad = own_grad.reshape(HEADS, rows, cols)
    term = jnp.einsum(
        "ijc,hij->hc", pair.astype(f32), own_grad, precision=lax.Precision.HIGHEST
    )
    term = sum([term] + [partner(term, s) for s in range(1, n_res)])
    rights = [rights, partner(rights, 1)]
    extra = jnp.stack([pair_bias_matrix.astype(f32).T, term])
    grads = list(grads)
    for s in (1, 3):
        grads[s] = peer(grads[s], s)
    early = [grads[s] for s in (1, 3)]
    near, extra, rights, early = lax.optimization_barrier((near, extra, rights, early))
    for s, piece in zip((1, 3), early):
        grads[s] = piece
    far = partner(near, 1)

    across = n_res // 2
    d_right = pl.pallas_call(
        functools.partial(d_right_kernel, n_seq, n_res),
        in_specs=[smem] + [vmem] * 4,
        out_shape=jax.ShapeDtypeStruct((n_seq, block * cols + 2 * HEADS, pair_channels), bf16),
        scratch_shapes=[
            pltpu.VMEM((HEADS, residues, residues), bf16),
        ],
        compiler_params=params,
        name="d_right",
    )((b % 2).reshape(1), near, far, extra, left)
    d_right = lax.all_to_all(d_right, "seq", 0, 0, tiled=True)

    piece = (2 * block, rows, pair_channels)
    d_left = pl.pallas_call(
        functools.partial(d_left_kernel, n_seq, n_res),
        in_specs=[smem] + [vmem] * 4,
        out_shape=[jax.ShapeDtypeStruct(piece, bf16)] * across,
        scratch_shapes=[
            pltpu.VMEM((across,) + piece, bf16),
            pltpu.VMEM((HEADS, across * rows, residues), bf16),
            pltpu.VMEM((2, block, residues, pair_channels), bf16),
        ],
        compiler_params=params,
        name="d_left",
    )(jnp.stack([b % 2, b // 2]).astype(jnp.int32), near, extra, *rights)
    d_left = list(d_left[:1]) + [partner(d_left[s], 2 * s) for s in range(1, across)]
    for s in range(1, groups):
        if s not in (1, 3):
            grads[s] = peer(grads[s], s)
    d_left, grads = lax.optimization_barrier((d_left, grads))
    query_gradient, key_gradient, value_gradient = pl.pallas_call(
        unpack_kernel,
        in_specs=[smem] + [vmem] * groups,
        out_shape=[jax.ShapeDtypeStruct(alignment_query.shape, bf16)] * 3,
        scratch_shapes=[pltpu.VMEM((groups,) + slots, bf16)],
        compiler_params=params,
        name="unpack",
    )(place.reshape(1), *grads)

    d_bias_weight, d_left, d_right = pl.pallas_call(
        functools.partial(place_kernel, inner),
        in_specs=[smem] + [vmem] * (1 + across),
        out_shape=[
            jax.ShapeDtypeStruct((HEADS, pair_channels), f32),
            jax.ShapeDtypeStruct((across * 2 * block, rows, pair_channels), bf16),
            jax.ShapeDtypeStruct((n_seq * block, cols, pair_channels), bf16),
        ],
        compiler_params=params,
        name="place",
    )((b // 2).reshape(1), d_right, *d_left)
    d_bias_weight = d_bias_weight.T
    return (query_gradient, key_gradient, value_gradient, d_bias_weight, d_left, d_right)


def solution(mesh):
    placed = (
        P(BOTH, None, None),
        P(BOTH, None, None),
        P(BOTH, None, None),
        P(BOTH, None, None),
        P(),
        P("res", "seq", None),
        P(),
        P("seq", "res", None),
        P("res", "seq", None),
    )
    return jax.shard_map(
        functools.partial(shards, mesh.shape["seq"], mesh.shape["res"]),
        mesh=mesh,
        in_specs=placed,
        out_specs=(
            P(BOTH, None, None),
            P(BOTH, None, None),
            P(BOTH, None, None),
            P(),
            P("seq", "res", None),
            P("res", "seq", None),
        ),
        check_vma=False,
    )
```

```python
import functools
import math

import jax
import jax.numpy as jnp
from jax import lax
from jax.experimental import pallas as pl
from jax.experimental.pallas import tpu as pltpu
from jax.sharding import PartitionSpec as P

HEADS = 8
HEAD_DIM = 32
BIG_NEGATIVE = -1e30
BOTH = ("seq", "res")
NT = (((1,), (1,)), ((), ()))
TN = (((0,), (0,)), ((), ()))

f32 = jnp.float32
bf16 = jnp.bfloat16


def attention_kernel(
    n_seq, n_res, groups, bias_ref, chain_ref, *refs
):
    arrays, grads = refs[:groups], refs[groups : 2 * groups]
    share_ref, masked, total = refs[2 * groups :]
    heads, residues, _ = masked.shape
    cols, rows = residues // n_seq, residues // n_res
    width = heads * HEAD_DIM
    scale = HEAD_DIM**-0.5

    chain_row = chain_ref[...].astype(f32)
    chain_col = jnp.broadcast_to(chain_row, (8, residues)).T[:, :1]
    for h in range(heads):
        for a in range(n_seq):
            band = jnp.concatenate(
                [bias_ref[a * n_res + b, :, h * rows : (h + 1) * rows] for b in range(n_res)],
                axis=-1,
            )
            allowed = chain_col[a * cols : (a + 1) * cols] == chain_row
            masked[h, a * cols : (a + 1) * cols, :] = jnp.where(allowed, band, BIG_NEGATIVE)
    total[...] = jnp.zeros_like(total)

    def sequence(x_ref, n):
        query_parts, key_parts, value_parts = [], [], []
        for h in range(heads):
            q, k, v, g = [
                x_ref[n, :, t * width + h * HEAD_DIM : t * width + (h + 1) * HEAD_DIM]
                for t in range(4)
            ]
            scores = lax.dot_general(k, q, NT, preferred_element_type=f32) * scale + masked[h]
            top = jnp.max(scores, axis=0, keepdims=True)
            expo = jnp.exp(scores - top)
            probs = expo * (1.0 / jnp.sum(expo, axis=0, keepdims=True))
            dprobs = lax.dot_general(v, g, NT, preferred_element_type=f32)
            dscores = probs * (dprobs - jnp.sum(probs * dprobs, axis=0, keepdims=True))
            total[h] += dscores
            dscores_b = dscores.astype(bf16)
            query_parts.append(
                lax.dot_general(dscores_b, k, TN, preferred_element_type=f32) * scale
            )
            key_parts.append(jnp.dot(dscores_b, q, preferred_element_type=f32) * scale)
            value_parts.append(jnp.dot(probs.astype(bf16), g, preferred_element_type=f32))
        return [
            jnp.concatenate(parts, axis=-1).astype(bf16)
            for parts in (query_parts, key_parts, value_parts)
        ]

    for s in range(groups):
        units = sum([sequence(arrays[s], n) for n in range(arrays[s].shape[0])], [])
        slots = grads[s].shape[0]
        each = len(units) // slots
        for n in range(slots):
            grads[s][n] = jnp.concatenate(units[n * each : (n + 1) * each], axis=-1)

    for a in range(n_seq):
        for b in range(n_res):
            share_ref[a * n_res + b] = jnp.concatenate(
                [
                    total[h, a * cols : (a + 1) * cols, b * rows : (b + 1) * rows]
                    for h in range(heads)
                ],
                axis=-1,
            ).astype(bf16)


def unpack_kernel(place_ref, *refs):
    pieces, outs, held = refs[:-4], refs[-4:-1], refs[-1]
    groups = len(pieces)
    own = outs[0].shape[0]
    slots, _, lanes = pieces[0].shape
    each = 3 * own // slots
    width = lanes // each
    for s in range(groups):
        held[s] = pieces[s][...]
    place = place_ref[0]
    for t in range(3):
        for n in range(own):
            slot, start = (3 * n + t) // each, (3 * n + t) % each * width
            outs[t][n] = jnp.concatenate(
                [held[place ^ g, slot, :, start : start + width] for g in range(groups)], axis=-1
            )


def pack_kernel(groups, n_res, scalars, *refs):
    arrays, (left_ref, right_ref), refs = refs[:4], refs[4:6], refs[6:]
    outs, triangles, held = refs[:groups], refs[groups:-1], refs[-1]
    place, b = scalars[0], scalars[1]
    block, rows = triangles[0].shape[1:3]
    cols = right_ref.shape[-2]
    width = held.shape[-1] // 4
    for g in range(groups):
        held[g] = jnp.concatenate(
            [x[:, :, g * width : (g + 1) * width] for x in arrays], axis=-1
        )
    for s in range(groups):
        outs[s][...] = held[place ^ s]
    for s in range(n_res):
        t = turn(b ^ s, n_res) * block
        triangles[s][0] = left_ref[pl.ds(t, block)]
        for y in range(rows // cols):
            triangles[s][1, :, y * cols : (y + 1) * cols] = right_ref[y, b ^ s]


def turn(b, n_res):
    return b % 2 * (n_res // 2) + b // 2


def order_rights_kernel(scalars, *refs):
    pieces, chunks_ref = refs[:-1], refs[-1]
    rows, cols = pieces[0].shape[2], chunks_ref.shape[2]
    each = rows // cols
    for s, piece in enumerate(pieces):
        for y in range(each):
            chunks_ref[(scalars[0] ^ s) * each + y] = piece[1, :, y * cols : (y + 1) * cols]


def order_lefts_kernel(scalars, *refs):
    pieces, left_ref = refs[:-1], refs[-1]
    rows = pieces[0].shape[2]
    for s, piece in enumerate(pieces):
        b = scalars[0] ^ s
        left_ref[:, pl.ds(pl.multiple_of(b * rows, rows), rows), :] = piece[0]


def pairs_of(block):
    return [(k, min(2, block - k)) for k in range(0, block, 2)]


def d_left_kernel(n_seq, n_res, scalars, near_ref, extra_ref, *refs):
    rights, outs = refs[:2], refs[2:-2]
    flat, right = refs[-2:]
    heads, count, residues = flat.shape
    held = heads // near_ref.shape[1]
    cols, rows = residues // n_seq, residues // n_res
    across = n_res // 2
    block = rights[0].shape[1]
    core, x = scalars[0], scalars[1]
    for part in range(2):
        where = core ^ part
        for a in range(n_seq):
            right[where, :, a * cols : (a + 1) * cols, :] = rights[part][a]
    for h in range(heads):
        group, place = h // held, h % held
        turned = jnp.concatenate(
            [
                jnp.concatenate(
                    [
                        near_ref[a * across + u, group, :, place * rows : (place + 1) * rows]
                        for u in range(across)
                    ],
                    axis=-1,
                )
                for a in range(n_seq)
            ],
            axis=0,
        )
        flat[h] = turned.astype(f32).T.astype(bf16)
    sums = outs[-1]
    channels = right.shape[-1]
    for c in range(2):
        for k, wide in pairs_of(block):
            both = jnp.concatenate([right[c, k + n] for n in range(wide)], axis=-1)
            row = jnp.zeros((count, wide * channels), f32)
            for h in range(heads):
                weight = jnp.concatenate([extra_ref[0, h : h + 1, :]] * wide, axis=-1)
                row += jnp.dot(flat[h], both, preferred_element_type=f32) * weight
            for n in range(wide):
                part = row[:, n * channels : (n + 1) * channels].astype(bf16)
                for u in range(across):
                    sums[u, c * block + k + n] = part[u * rows : (u + 1) * rows]
    for s in range(across):
        outs[s][...] = sums[x ^ s]


def d_right_kernel(n_seq, n_res, scalars, near_ref, far_ref, extra_ref, left, out, turned):
    heads, residues, _ = turned.shape
    held = heads // near_ref.shape[1]
    cols, rows = residues // n_seq, residues // n_res
    across = n_res // 2
    block = left.shape[0]
    core = scalars[0]
    for h in range(heads):
        group, place = h // held, h % held
        for a in range(n_seq):
            band = []
            for b in range(n_res):
                piece = (
                    a * across + b // 2, group, slice(None), slice(place * rows, (place + 1) * rows)
                )
                band.append(jnp.where(core == b % 2, near_ref[piece], far_ref[piece]))
            turned[h, a * cols : (a + 1) * cols, :] = jnp.concatenate(band, axis=-1)
    channels = left.shape[-1]
    for k, wide in pairs_of(block):
        both = jnp.concatenate([left[k + n] for n in range(wide)], axis=-1)
        row = jnp.zeros((residues, wide * channels), f32)
        for h in range(heads):
            weight = jnp.concatenate([extra_ref[0, h : h + 1, :]] * wide, axis=-1)
            row += jnp.dot(turned[h], both, preferred_element_type=f32) * weight
        for n in range(wide):
            part = row[:, n * channels : (n + 1) * channels].astype(bf16)
            for a in range(n_seq):
                out[a, (k + n) * cols : (k + n + 1) * cols] = part[a * cols : (a + 1) * cols]
    term = extra_ref[1]
    high = term.astype(bf16).astype(f32)
    both = jnp.concatenate([high, term - high], axis=0).astype(bf16)
    for a in range(n_seq):
        out[a, block * cols :] = both


def place_kernel(inner, scalars, received_ref, *refs):
    pieces, (term_ref, left_ref, right_ref) = refs[:-3], refs[-3:]
    heads = term_ref.shape[0]
    sources, size, _ = received_ref.shape
    cols = right_ref.shape[1]
    block = right_ref.shape[0] // sources
    total = jnp.zeros_like(term_ref)
    for a in range(sources):
        both = received_ref[a, block * cols :].astype(f32)
        total += both[:heads] + both[heads:]
        p = a % inner * (sources // inner) + a // inner
        for k in range(block):
            right_ref[p * block + k] = received_ref[a, k * cols : (k + 1) * cols]
    term_ref[...] = total
    size = pieces[0].shape[0]
    for s, piece in enumerate(pieces):
        left_ref[pl.ds(pl.multiple_of((scalars[0] ^ s) * size, size), size)] = piece[...]


def shards(
    n_seq,
    n_res,
    alignment_query,
    alignment_key,
    attended_vectors,
    attended_cotangent,
    chain_index_per_residue,
    pair,
    pair_bias_matrix,
    left_operand_input,
    right_operand_input,
):
    own, residues, channels = alignment_query.shape
    devices = n_seq * n_res
    spread = 2 - n_seq % 2, 2 - n_res % 2
    groups = spread[0] * spread[1]
    held = HEADS // groups
    width = held * HEAD_DIM
    rows, cols, pair_channels = pair.shape
    block = residues // devices
    a, b = lax.axis_index("seq"), lax.axis_index("res")
    flat = a * n_res + b

    bias = jnp.einsum("ijc,ch->hij", pair, pair_bias_matrix, preferred_element_type=f32)
    bias = bias.reshape(groups, held, rows, cols).transpose(0, 3, 1, 2)
    bias = bias.reshape(1, spread[0], 1, spread[1], cols, held * rows)
    by_group = (n_seq // spread[0], spread[0], n_res // spread[1], spread[1], cols, held * rows)
    bias = jnp.broadcast_to(bias, by_group)
    bias = lax.all_to_all(
        bias.reshape(devices, cols, held * rows), BOTH, 0, 0, tiled=True
    )

    place = a % spread[0] * spread[1] + b % spread[1]
    smem, vmem = [pl.BlockSpec(memory_space=s) for s in (pltpu.SMEM, pltpu.VMEM)]
    params = pltpu.CompilerParams(vmem_limit_bytes=12 * 1024 * 1024)
    packed = (own, residues, 4 * width)
    right_parts = (n_seq // n_res, n_res, block, cols, pair_channels)
    pieces = pl.pallas_call(
        functools.partial(pack_kernel, groups, n_res),
        in_specs=[smem] + [vmem] * 6,
        out_shape=[jax.ShapeDtypeStruct(packed, bf16)] * groups
        + [jax.ShapeDtypeStruct((2, block, rows, pair_channels), bf16)] * n_res,
        scratch_shapes=[
            pltpu.VMEM((groups,) + packed, bf16),
        ],
        compiler_params=params,
        name="pack",
    )(
        jnp.stack([place, b]).astype(jnp.int32),
        alignment_query,
        alignment_key,
        attended_vectors,
        attended_cotangent,
        left_operand_input,
        right_operand_input.reshape(right_parts),
    )
    arrays, triangles = pieces[:groups], pieces[groups:]

    def peer(x, s):
        pairs = [
            (d, (d // n_res ^ s // spread[1]) * n_res + (d % n_res ^ s % spread[1]))
            for d in range(devices)
        ]
        return lax.ppermute(x, BOTH, pairs)

    def partner(x, s):
        return lax.ppermute(x, "res", [(i, i ^ s) for i in range(n_res)])

    arrays = list(arrays[:1]) + [peer(arrays[s], s) for s in range(1, groups)]

    inner = 2 - n_seq % 2
    half = n_seq // inner
    triangles = list(triangles[:1]) + [partner(triangles[s], s) for s in range(1, n_res)]
    arrays, triangles = lax.optimization_barrier((arrays, triangles))
    rights = pl.pallas_call(
        order_rights_kernel,
        in_specs=[smem] + [vmem] * n_res,
        out_shape=jax.ShapeDtypeStruct((n_seq, block, cols, pair_channels), bf16),
        compiler_params=params,
        name="order_rights",
    )(b.reshape(1), *triangles)
    left = pl.pallas_call(
        order_lefts_kernel,
        in_specs=[smem] + [vmem] * n_res,
        out_shape=jax.ShapeDtypeStruct((block, residues, pair_channels), bf16),
        compiler_params=params,
        name="order_lefts",
    )(b.reshape(1), *triangles)
    pairs = []
    for d in range(devices):
        g = d // n_res * n_res + turn(d % n_res, n_res)
        p = g % n_seq
        pairs.append((d, (p % half * inner + p // half) * n_res + g // n_seq))
    left = lax.ppermute(left, BOTH, pairs)
    rights = lax.all_to_all(rights, "seq", 0, 0, tiled=True)

    each = max(1, 128 // width)
    slots = (3 * own // each, residues, each * width)
    outs = pl.pallas_call(
        functools.partial(attention_kernel, n_seq, n_res, groups),
        out_shape=[jax.ShapeDtypeStruct(slots, bf16)] * groups
        + [jax.ShapeDtypeStruct(bias.shape, bf16)],
        scratch_shapes=[pltpu.VMEM((held, residues, residues), f32)] * 2,
        compiler_params=params,
        cost_estimate=pl.CostEstimate(flops=4 * 10**9, bytes_accessed=0, transcendentals=0),
        name="attention",
    )(bias, chain_index_per_residue.reshape(1, residues), *arrays)
    grads, share = outs[:groups], outs[groups]

    share, rights = lax.optimization_barrier((share, rights))
    share = lax.all_to_all(share, BOTH, 0, 0, tiled=True)
    share, left = lax.optimization_barrier((share, left))
    share = jnp.sum(share.astype(f32).reshape(by_group), axis=(0, 2))
    share = share.reshape(groups, cols, held * rows)
    parity = [list(range(c, devices, 2)) for c in range(2)]
    near = jnp.broadcast_to(share.astype(bf16)[None], (devices // 2,) + share.shape)
    near = lax.all_to_all(near, BOTH, 0, 0, axis_index_groups=parity, tiled=True)
    own_grad = share.reshape(groups, cols, held, rows).transpose(0, 2, 3, 1)
    own_grad = own_grad.reshape(HEADS, rows, cols)
    term = jnp.einsum(
        "ijc,hij->hc", pair.astype(f32), own_grad, precision=lax.Precision.HIGHEST
    )
    term = sum([term] + [partner(term, s) for s in range(1, n_res)])
    rights = [rights, partner(rights, 1)]
    extra = jnp.stack([pair_bias_matrix.astype(f32).T, term])
    grads = list(grads)
    for s in (1, 3):
        grads[s] = peer(grads[s], s)
    early = [grads[s] for s in (1, 3)]
    near, extra, rights, early = lax.optimization_barrier((near, extra, rights, early))
    for s, piece in zip((1, 3), early):
        grads[s] = piece
    far = partner(near, 1)

    across = n_res // 2
    d_right = pl.pallas_call(
        functools.partial(d_right_kernel, n_seq, n_res),
        in_specs=[smem] + [vmem] * 4,
        out_shape=jax.ShapeDtypeStruct((n_seq, block * cols + 2 * HEADS, pair_channels), bf16),
        scratch_shapes=[
            pltpu.VMEM((HEADS, residues, residues), bf16),
        ],
        compiler_params=params,
        name="d_right",
    )((b % 2).reshape(1), near, far, extra, left)
    d_right = lax.all_to_all(d_right, "seq", 0, 0, tiled=True)

    piece = (2 * block, rows, pair_channels)
    d_left = pl.pallas_call(
        functools.partial(d_left_kernel, n_seq, n_res),
        in_specs=[smem] + [vmem] * 4,
        out_shape=[jax.ShapeDtypeStruct(piece, bf16)] * across,
        scratch_shapes=[
            pltpu.VMEM((across,) + piece, bf16),
            pltpu.VMEM((HEADS, across * rows, residues), bf16),
            pltpu.VMEM((2, block, residues, pair_channels), bf16),
        ],
        compiler_params=params,
        name="d_left",
    )(jnp.stack([b % 2, b // 2]).astype(jnp.int32), near, extra, *rights)
    d_left = list(d_left[:1]) + [partner(d_left[s], 2 * s) for s in range(1, across)]
    for s in range(1, groups):
        if s not in (1, 3):
            grads[s] = peer(grads[s], s)
    d_left, grads = lax.optimization_barrier((d_left, grads))
    query_gradient, key_gradient, value_gradient = pl.pallas_call(
        unpack_kernel,
        in_specs=[smem] + [vmem] * groups,
        out_shape=[jax.ShapeDtypeStruct(alignment_query.shape, bf16)] * 3,
        scratch_shapes=[pltpu.VMEM((groups,) + slots, bf16)],
        compiler_params=params,
        name="unpack",
    )(place.reshape(1), *grads)

    d_bias_weight, d_left, d_right = pl.pallas_call(
        functools.partial(place_kernel, inner),
        in_specs=[smem] + [vmem] * (1 + across),
        out_shape=[
            jax.ShapeDtypeStruct((HEADS, pair_channels), f32),
            jax.ShapeDtypeStruct((across * 2 * block, rows, pair_channels), bf16),
            jax.ShapeDtypeStruct((n_seq * block, cols, pair_channels), bf16),
        ],
        compiler_params=params,
        name="place",
    )((b // 2).reshape(1), d_right, *d_left)
    d_bias_weight = d_bias_weight.T
    return (query_gradient, key_gradient, value_gradient, d_bias_weight, d_left, d_right)


def solution(mesh):
    placed = (
        P(BOTH, None, None),
        P(BOTH, None, None),
        P(BOTH, None, None),
        P(BOTH, None, None),
        P(),
        P("res", "seq", None),
        P(),
        P("seq", "res", None),
        P("res", "seq", None),
    )
    return jax.shard_map(
        functools.partial(shards, mesh.shape["seq"], mesh.shape["res"]),
        mesh=mesh,
        in_specs=placed,
        out_specs=(
            P(BOTH, None, None),
            P(BOTH, None, None),
            P(BOTH, None, None),
            P(),
            P("seq", "res", None),
            P("res", "seq", None),
        ),
        check_vma=False,
    )
```
